512 devices in a mesh: panel: 32 (over y, z_lo), col: 8 (over z_hi, x), layer: 2 (over core).
Axes of the slice: x: 4, y: 8, z: 8 (z_hi: 2, z_lo: 4; z = z_hi * 4 + z_lo), core: 2. Of those that a mesh axis runs over, the one named last changes fastest.
Arguments:
- iterate: bfloat16 [8192, 4096], P(('layer', 'panel'), 'col'), parts along dimension 0, may hold values from -3 to 3
Outputs:
- next_iterate: bfloat16 [8192, 4096], P(('layer', 'panel'), 'col'), parts along dimension 0
The draws below stay inside these ranges and needn't reach their ends.
There are 2 independent parts, one for each index of `layer`. The reference program is written for one: setup_inputs(seed, part) draws one part's arguments, and reference() takes and returns one part's arrays. A program takes and returns all parts, laid end to end along the dimension named above; each array names one. Nothing has to cross between parts.
All inputs are finite; a program needn't handle non-finite values.
Results may differ from the reference program's by a relative error of at most 0.015.
Values may be sent and summed in bfloat16 or wider, within the bound.
A program may use at most 64 MiB of HBM per device.

```python
import jax
import jax.numpy as jnp

ROWS = 4096
COLS = 4096


def steps_of(own_key, dims, shards, smallest, largest):
    loudness, own = 1.0, jax.random.fold_in(own_key, 6)
    for dim, shards_of in shards:
        draws = jnp.exp(jax.random.uniform(jax.random.fold_in(own, dim), (shards_of,), jnp.float32, smallest / len(shards), largest / len(shards)))
        loudness = loudness * jnp.repeat(draws, dims[dim] // shards_of).reshape([-1 if axis == dim else 1 for axis in range(len(dims))])
    return loudness


def gaussian(rng, shape, width, limit, pieces=(), held_as=jnp.bfloat16):
    array = width * jax.random.normal(rng, shape, jnp.float32)
    if pieces:
        array = array * steps_of(rng, shape, pieces, -0.22, 0.18)
    return jnp.clip(array, -limit, limit).astype(held_as)


def setup_inputs(seed: int = 0, part: int = 0) -> dict:
    keys = jax.random.split(jax.random.key(seed), 2)
    part_keys = jax.random.split(jax.random.fold_in(keys[1], part), 2)
    iterate = gaussian(part_keys[0], (ROWS, COLS), 0.5, 3.0, ((0, 32), (1, 8)))
    return dict(iterate=iterate)


def reference(iterate):
    gram = (jnp.dot(iterate, iterate.T, preferred_element_type=jnp.float32) / COLS).astype(jnp.bfloat16)
    first = jnp.dot(gram, iterate, preferred_element_type=jnp.float32)
    first_rounded = first.astype(jnp.bfloat16)
    second = jnp.dot(gram, first_rounded, preferred_element_type=jnp.float32)
    result = 3.4445 * iterate.astype(jnp.float32) - 4.7750 * first + 2.0315 * second
    return result.astype(jnp.bfloat16)
```

```python
import functools

import jax
import jax.numpy as jnp
from jax import lax
from jax.experimental import pallas as pl
from jax.experimental.pallas import tpu as pltpu
from jax.sharding import PartitionSpec as P

NX, N, NLO = 4, 8, 4
HALF = N // 2
ROWS, COLS = 64, 1024
MESH = pl.DeviceIdType.MESH
UPTO = 99


def kernel(x_ref, o_ref, w, p, q, gp, gr, g, fp, fr, f, sp, sr, first, ow,
           ex_sem, p_sem, q_sem, gr_sem, g_sem, fr_sem, f_sem, sr_sem, out_sem):
    panel, col, layer = lax.axis_index("panel"), lax.axis_index("col"), lax.axis_index("layer")
    y, z_lo = panel // NLO, panel % NLO
    z_hi, x = col // NX, col % NX
    z = z_hi * NLO + z_lo

    def device(x, y, z):
        return (y * NLO + z % NLO, (z // NLO) * NX + x, layer)

    def peer1(d):
        return device(x, (y + d * layer) % N, (z + d * (1 - layer)) % N)

    def peer2(d):
        return device(x, (y + d * (1 - layer)) % N, (z + d * layer) % N)

    def peer_x(d):
        return device((x + d) % NX, y, z)

    partner = device(x, y, (z + HALF) % N)
    pos1 = z * (1 - layer) + y * layer
    pos2 = y * (1 - layer) + z * layer

    barrier = pltpu.get_barrier_semaphore()
    for d in range(1, N):
        pl.semaphore_signal(barrier, inc=1, device_id=peer1(d), device_id_type=MESH)
        pl.semaphore_signal(barrier, inc=1, device_id=peer2(d), device_id_type=MESH)
    for d in range(1, NX):
        pl.semaphore_signal(barrier, inc=1, device_id=peer_x(d), device_id_type=MESH)
    pl.semaphore_wait(barrier, 2 * (N - 1) + NX - 1)

    def send(src, dst, sems, k, to):
        copy = pltpu.make_async_remote_copy(
            src_ref=src, dst_ref=dst, send_sem=sems.at[0, k], recv_sem=sems.at[1, k],
            device_id=to, device_id_type=MESH)
        copy.start()
        return copy

    started = []

    mine = pl.multiple_of(z_hi * ROWS, ROWS)
    other = pl.multiple_of((1 - z_hi) * ROWS, ROWS)
    mine_c = pl.multiple_of(z_hi * 512, 512)
    other_c = pl.multiple_of((1 - z_hi) * 512, 512)
    if UPTO >= 1:
        ex = send(x_ref.at[pl.ds(other, ROWS), :], w.at[:, pl.ds(mine_c, 512)], ex_sem, 0, partner)
        w[:, pl.ds(mine_c, 512)] = x_ref[pl.ds(mine, ROWS), :]
        ex.wait()

    def gather_steps(src, buf, sems, pos, peer):
        right, left = peer(1), peer(N - 1)
        prev = None
        for s in range(1, HALF + 1):
            if prev is not None:
                prev[0].wait_recv()
            a = src if s == 1 else buf.at[(pos + N - s + 1) % N]
            da = buf.at[(pos + N - s + 1) % N]
            b = src if s == 1 else buf.at[(pos + s - 1) % N]
            db = buf.at[(pos + s - 1) % N]
            if s == HALF:
                a, da = a.at[pl.ds(0, ROWS // 2), :], da.at[pl.ds(0, ROWS // 2), :]
                b, db = b.at[pl.ds(ROWS // 2, ROWS // 2), :], db.at[pl.ds(ROWS // 2, ROWS // 2), :]
            ca = send(a, da, sems, 2 * s - 2, right)
            if prev is not None:
                prev[1].wait_recv()
            cb = send(b, db, sems, 2 * s - 1, left)
            prev = (ca, cb)
            started.extend(prev)
            yield
        prev[0].wait_recv()
        prev[1].wait_recv()
        yield

    def run(*gens):
        gens = list(gens)
        for _ in range(HALF + 1):
            for gen in gens:
                next(gen)

    if UPTO >= 2:
        run(gather_steps(w, p, p_sem, pos1, peer1), gather_steps(w, q, q_sem, pos2, peer2))
        p[pos1] = w[...]
        q[pos2] = w[...]

    if UPTO >= 3:
        pm = p[...].reshape(N * ROWS, COLS)
        qm = q[...].reshape(N * ROWS, COLS)
        gp[...] = lax.dot_general(pm, qm, (((1,), (1,)), ((), ())), preferred_element_type=jnp.float32
                                  ).astype(jnp.bfloat16).reshape(gp.shape)
        copies = [send(gp.at[(x + d) % NX], gr.at[d - 1], gr_sem, d - 1, peer_x(d)) for d in range(1, NX)]
        total = gp[x].astype(jnp.float32)
        for d, c in enumerate(copies):
            c.wait_recv()
            total += gr[d].astype(jnp.float32)
        started.extend(copies)
        g[x] = (total * (1.0 / 4096)).astype(jnp.bfloat16)
    if UPTO >= 4:
        copies = [send(g.at[x], g.at[x], g_sem, d - 1, peer_x(d)) for d in range(1, NX)]
        for c in copies:
            c.wait_recv()
        started.extend(copies)

    def scatter(parts, got, sems, pos, peer):
        copies = [send(parts.at[(pos + d) % N], got.at[d - 1], sems, d - 1, peer(d)) for d in range(1, N)]
        total = parts[pos].astype(jnp.float32)
        for d, c in enumerate(copies):
            c.wait_recv()
            total += got[d].astype(jnp.float32)
        started.extend(copies)
        return total

    if UPTO >= 5:
        gm = g[...].reshape(N * ROWS, N * ROWS)
        fp[...] = jnp.dot(gm, q[...].reshape(N * ROWS, COLS), preferred_element_type=jnp.float32
                          ).astype(jnp.bfloat16).reshape(fp.shape)
        first[...] = scatter(fp, fr, fr_sem, pos1, peer1)
        f[pos1] = first[...].astype(jnp.bfloat16)
    if UPTO >= 6:
        run(gather_steps(f.at[pos1], f, f_sem, pos1, peer1))
    if UPTO >= 7:
        gm = g[...].reshape(N * ROWS, N * ROWS)
        fm = f[...].reshape(N * ROWS, COLS)
        sp[...] = lax.dot_general(gm, fm, (((0,), (0,)), ((), ())), preferred_element_type=jnp.float32
                                  ).astype(jnp.bfloat16).reshape(sp.shape)
        second = scatter(sp, sr, sr_sem, pos2, peer2)
        ow[...] = (3.4445 * w[...].astype(jnp.float32) - 4.775 * first[...] + 2.0315 * second).astype(jnp.bfloat16)
    if UPTO >= 8:
        out = send(ow.at[:, pl.ds(other_c, 512)], o_ref.at[pl.ds(mine, ROWS), :], out_sem, 0, partner)
        o_ref[pl.ds(mine, ROWS), :] = ow[:, pl.ds(mine_c, 512)]
        out.wait()
    else:
        o_ref[...] = x_ref[...]
    for c in started:
        c.wait_send()


def body(iterate):
    bf, f32 = jnp.bfloat16, jnp.float32
    stack = pltpu.VMEM((N, ROWS, COLS), bf)
    gram = pltpu.VMEM((NX, N * ROWS // NX, N * ROWS), bf)
    dma = lambda n: pltpu.SemaphoreType.DMA((2, n))
    return pl.pallas_call(
        kernel,
        out_shape=jax.ShapeDtypeStruct(iterate.shape, bf),
        in_specs=[pl.BlockSpec(memory_space=pltpu.VMEM)],
        out_specs=pl.BlockSpec(memory_space=pltpu.VMEM),
        scratch_shapes=[
            pltpu.VMEM((ROWS, COLS), bf), stack, stack,
            gram, pltpu.VMEM((NX - 1, N * ROWS // NX, N * ROWS), bf), gram,
            stack, pltpu.VMEM((N - 1, ROWS, COLS), bf), stack,
            stack, pltpu.VMEM((N - 1, ROWS, COLS), bf),
            pltpu.VMEM((ROWS, COLS), f32), pltpu.VMEM((ROWS, COLS), bf),
            dma(1), dma(N), dma(N), dma(NX - 1), dma(NX - 1), dma(N - 1), dma(N), dma(N - 1), dma(1),
        ],
        compiler_params=pltpu.CompilerParams(
            collective_id=0, has_side_effects=True, vmem_limit_bytes=40 * 1024 * 1024),
    )(iterate)


def solution(mesh):
    return jax.shard_map(
        body, mesh=mesh,
        in_specs=(P(("layer", "panel"), "col"),),
        out_specs=P(("layer", "panel"), "col"),
        check_vma=False,
    )
```

```python
import jax
import jax.numpy as jnp
from jax import lax
from jax.experimental import pallas as pl
from jax.experimental.pallas import tpu as pltpu
from jax.sharding import PartitionSpec as P

NX, N, NLO = 4, 8, 4
HALF = N // 2
ROWS, COLS = 64, 512
PART = COLS // 2
MESH = pl.DeviceIdType.MESH
BF, F32 = jnp.bfloat16, jnp.float32
UPTO = 99
FLIP = 1


def kernel(x_ref, o_ref, ab, acc, gp, gr, g, gt, fp, fr, f, first, sp, sr0, sr1, ow,
           ex_sem, a_sem, b_sem, gr_sem, g_sem, fr_sem, f_sem, sr_sem, out_sem):
    panel, col, layer = lax.axis_index("panel"), lax.axis_index("col"), lax.axis_index("layer")
    y, z_lo = panel // NLO, panel % NLO
    z_hi, x = col // NX, col % NX
    z = z_hi * NLO + z_lo
    o = 1 - layer if FLIP else layer

    def device(x, y, z):
        return (y * NLO + z % NLO, (z // NLO) * NX + x, layer)

    def unplace(t):
        return (t % 2) * NLO + t // 2

    def ring1(t):
        return device(x, y + o * (t - y), z + (1 - o) * (unplace(t) - z))

    def ring2(t):
        return device(x, y + (1 - o) * (t - y), z + o * (unplace(t) - z))

    def peer_x(d):
        return device((x + d) % NX, y, z)

    placed = z_lo * 2 + z_hi
    own1 = (1 - o) * placed + o * y
    own2 = (1 - o) * y + o * placed
    partner = device(x, y, (z + HALF) % N)

    barrier = pltpu.get_barrier_semaphore()
    for d in range(1, N):
        pl.semaphore_signal(barrier, inc=1, device_id=device(x, (y + d) % N, z), device_id_type=MESH)
        pl.semaphore_signal(barrier, inc=1, device_id=device(x, y, (z + d) % N), device_id_type=MESH)
    for d in range(1, NX):
        pl.semaphore_signal(barrier, inc=1, device_id=peer_x(d), device_id_type=MESH)
    pl.semaphore_wait(barrier, 2 * (N - 1) + NX - 1)

    def remote(src, dst, send_sem, recv_sem, to):
        return pltpu.make_async_remote_copy(
            src_ref=src, dst_ref=dst, send_sem=send_sem, recv_sem=recv_sem, device_id=to, device_id_type=MESH)

    started = []

    def send(src, dst, send_sem, recv_sem, to):
        copy = remote(src, dst, send_sem, recv_sem, to)
        copy.start()
        started.append(copy)
        return copy

    mine = pl.multiple_of(z_hi * ROWS, ROWS)
    other = pl.multiple_of((1 - z_hi) * ROWS, ROWS)

    exchange = send(x_ref.at[pl.ds(other, ROWS), :], ab.at[1 - o, z_hi, y], ex_sem.at[0, 0], ex_sem.at[1, 0], partner)

    sent = {}

    def along(ring, step, u):
        for way in (0, 1):
            if step == HALF and way != u:
                continue
            if step > 1:
                sent[ring, step - 1, u, way].wait_recv()
            back = 1 - step if way == 0 else step - 1
            if ring == 0:
                zz = (z + back + N) % N
                slot = ab.at[o, zz // NLO, (zz % NLO) * 2 + u]
                src = x_ref.at[pl.ds(u * ROWS, ROWS), :] if step == 1 else slot
                to = device(x, y, (z + (1 if way == 0 else N - 1)) % N)
                sems = a_sem
            else:
                yy = (y + back + N) % N
                slot = ab.at[1 - o, z_hi if u == 0 else 1 - z_hi, yy]
                src = x_ref.at[pl.ds(mine, ROWS), :] if step == 1 and u == 0 else slot
                to = device(x, (y + (1 if way == 0 else N - 1)) % N, z)
                sems = b_sem
            k = (step - 1) * 4 + u * 2 + way
            sent[ring, step, u, way] = send(src, slot, sems.at[0, k], sems.at[1, k], to)

    def arrived(ring, u):
        sent[ring, HALF, u, u].wait_recv()
        sent[ring, HALF - 1, u, 1 - u].wait_recv()

    for a in ((0, 1, 0), (1, 1, 0), (0, 1, 1)):
        along(*a)
    for u in (0, 1):
        ab[o, z_hi, z_lo * 2 + u] = x_ref[u * ROWS:(u + 1) * ROWS, :]
    ab[1 - o, z_hi, y] = x_ref[pl.ds(mine, ROWS), :]
    for a in ((0, 2, 0), (1, 2, 0), (0, 2, 1)):
        along(*a)
    exchange.wait_recv()
    for a in ((1, 1, 1), (0, 3, 0), (1, 3, 0), (0, 3, 1), (1, 2, 1), (0, 4, 0), (1, 4, 0), (0, 4, 1), (1, 3, 1), (1, 4, 1)):
        along(*a)
    arrived(0, 0)
    arrived(0, 1)
    arrived(1, 0)

    def nt(a, b):
        return lax.dot_general(a, b, (((1,), (1,)), ((), ())), preferred_element_type=F32)

    rows_all, rows_half = N * ROWS, HALF * ROWS
    acc[...] = nt(ab[0, z_hi].reshape(rows_all, COLS), ab[1, z_hi].reshape(rows_all, COLS))
    arrived(1, 1)

    own_half = own1 // HALF
    halves = (1 - own_half, own_half)
    c_late = 1 - z_hi
    if UPTO >= 3:
        gr_copies = []
        for k, half in enumerate(halves):
            at = pl.multiple_of(half * rows_half, rows_half)
            block = acc[pl.ds(at, rows_half), :] + nt(
                ab[0, c_late, pl.ds(half * HALF, HALF)].reshape(rows_half, COLS), ab[1, c_late].reshape(rows_all, COLS))
            gp[pl.ds(half * HALF, HALF)] = block.astype(BF).reshape(HALF, ROWS, rows_all)
            gr_copies.append([
                send(gp.at[half * HALF + (x + d) % NX], gr.at[k, d - 1], gr_sem.at[0, k * 3 + d - 1],
                     gr_sem.at[1, k * 3 + d - 1], peer_x(d)) for d in (2, 1, 3)])
        g_copies = []
        for k, half in enumerate(halves):
            mine_g = half * HALF + x
            for c in gr_copies[k]:
                c.wait_recv()
            total = gp[mine_g].astype(F32)
            for d in range(NX - 1):
                total += gr[k, d].astype(F32)
            g[mine_g] = (total * (1.0 / 4096)).astype(BF)
            g_copies.append([
                send(g.at[mine_g], g.at[mine_g], g_sem.at[0, k * 3 + d - 1], g_sem.at[1, k * 3 + d - 1], peer_x(d))
                for d in (2, 1, 3)])
    if UPTO >= 5:
        def send_first(v, k, half):
            for e in range(k, HALF):
                t = half * HALF + (own1 + e) % HALF
                send(fp.at[v, t], fr.at[v, own1], fr_sem.at[0, v * N + t], fr_sem.at[1, v * N + own1], ring1(t))

        for k, half in enumerate(halves):
            for c in g_copies[k]:
                c.wait_recv()
            rows = g[pl.ds(half * HALF, HALF)].reshape(rows_half, rows_all)
            for v in (0, 1):
                for c in (0, 1):
                    right = ab[1, c, :, :, v * PART:(v + 1) * PART].reshape(rows_all, PART)
                    fp[v, pl.ds(half * HALF, HALF), :, c * PART:(c + 1) * PART] = jnp.dot(
                        rows, right, preferred_element_type=F32).astype(BF).reshape(HALF, ROWS, PART)
                if v == 0:
                    send_first(v, k, half)
        for k, half in enumerate(halves):
            send_first(1, k, half)
        gt[...] = g[...].reshape(rows_all, rows_all).T

        others1 = [(own1 + e) % N for e in range(1, N)]
        others2 = [(own2 + e) % N for e in range(1, N)]
        for v in (0, 1):
            fr[v, own1] = fp[v, own1]
            for t in others1:
                remote(fr.at[v, t], fr.at[v, t], fr_sem.at[0, v * N + t], fr_sem.at[1, v * N + t], ring1(t)).wait_recv()
            total = fr[v, 0].astype(F32)
            for t in range(1, N):
                total += fr[v, t].astype(F32)
            first[v] = total
            f[v, own1] = total.astype(BF)
            if UPTO >= 6:
                for t in others1:
                    send(f.at[v, own1], f.at[v, own1], f_sem.at[0, v * N + t], f_sem.at[1, v * N + own1], ring1(t))

    if UPTO >= 7:
        rows2 = pl.multiple_of(own2 * ROWS, ROWS)

        def second_copy(v, t, way):
            sems = (sr_sem.at[0, v * N + t], sr_sem.at[1, v * N + own2])
            if way == 0:
                return remote(sp.at[v, t], sr0.at[v, own2], *sems, ring2(t))
            zz = unplace(t)
            return remote(sp.at[v, pl.ds((zz % NLO) * 2, 2), :, pl.ds(pl.multiple_of((zz // NLO) * PART, PART), PART)],
                          sr1.at[v, own2], *sems, ring2(t))

        def second_came(v, t, way):
            slot = (sr0, sr1)[way].at[v, t]
            return remote(slot, slot, sr_sem.at[0, v * N + t], sr_sem.at[1, v * N + t], ring2(t))

        for v in (0, 1):
            for t in others1:
                remote(f.at[v, t], f.at[v, t], f_sem.at[0, v * N + t], f_sem.at[1, v * N + t], ring1(t)).wait_recv()
            second = 2.0315 * jnp.dot(gt[...], f[v].reshape(rows_all, COLS), preferred_element_type=F32)
            sp[v] = second.astype(BF).reshape(N, ROWS, COLS)
            sp[v, own2] = (sp[v, own2].astype(F32) - 4.775 * first[v]).astype(BF)
            for way in (0, 1):
                @pl.when(o == way)
                def _():
                    for t in others2:
                        second_copy(v, t, way).start()
                    if way == 0:
                        sr0[v, own2] = sp[v, own2]
                    else:
                        sr1[v, own2] = sp[v, pl.ds(z_lo * 2, 2), :, pl.ds(pl.multiple_of(z_hi * PART, PART), PART)]

        def out_copy(v):
            return remote(ow.at[v, :, pl.ds(pl.multiple_of((1 - z_hi) * PART, PART), PART)],
                          o_ref.at[pl.ds(mine, ROWS), v * PART:(v + 1) * PART],
                          out_sem.at[0, v], out_sem.at[1, v], partner)

        @pl.when(o == 0)
        def _():
            for v in (0, 1):
                for t in others2:
                    second_came(v, t, 0).wait_recv()
                total = sr0[v, 0].astype(F32)
                for t in range(1, N):
                    total += sr0[v, t].astype(F32)
                for c in (0, 1):
                    own = ab[1, c, y, :, v * PART:(v + 1) * PART]
                    ow[v, :, c * PART:(c + 1) * PART] = (
                        3.4445 * own.astype(F32) + total[:, c * PART:(c + 1) * PART]).astype(BF)
                out_copy(v).start()
                o_ref[pl.ds(mine, ROWS), v * PART:(v + 1) * PART] = ow[
                    v, :, pl.ds(pl.multiple_of(z_hi * PART, PART), PART)]
            for v in (0, 1):
                for t in others2:
                    second_copy(v, t, 0).wait_send()
                out_copy(v).wait()

        @pl.when(o == 1)
        def _():
            for v in (0, 1):
                for t in others2:
                    second_came(v, t, 1).wait_recv()
                for h in (0, 1):
                    total = sr1[v, 0, h].astype(F32)
                    for t in range(1, N):
                        total += sr1[v, t, h].astype(F32)
                    own = x_ref[h * ROWS:(h + 1) * ROWS, v * PART:(v + 1) * PART]
                    o_ref[h * ROWS:(h + 1) * ROWS, v * PART:(v + 1) * PART] = (
                        3.4445 * own.astype(F32) + total).astype(BF)
            for v in (0, 1):
                for t in others2:
                    second_copy(v, t, 1).wait_send()
    else:
        o_ref[...] = x_ref[...]
    for c in started:
        c.wait_send()


def body(iterate):
    stack = pltpu.VMEM((2, N, ROWS, COLS), BF)
    gram = pltpu.VMEM((N, ROWS, N * ROWS), BF)
    dma = lambda n: pltpu.SemaphoreType.DMA((2, n))
    return pl.pallas_call(
        kernel,
        out_shape=jax.ShapeDtypeStruct(iterate.shape, BF),
        in_specs=[pl.BlockSpec(memory_space=pltpu.VMEM)],
        out_specs=pl.BlockSpec(memory_space=pltpu.VMEM),
        scratch_shapes=[
            pltpu.VMEM((2, 2, N, ROWS, COLS), BF),
            pltpu.VMEM((N * ROWS, N * ROWS), F32),
            gram, pltpu.VMEM((2, NX - 1, ROWS, N * ROWS), BF), gram,
            pltpu.VMEM((N * ROWS, N * ROWS), BF),
            stack, stack, stack,
            pltpu.VMEM((2, ROWS, COLS), F32),
            stack, stack, pltpu.VMEM((2, N, 2, ROWS, PART), BF),
            pltpu.VMEM((2, ROWS, COLS), BF),
            dma(1), dma(16), dma(16), dma(6), dma(6), dma(16), dma(16), dma(16), dma(2),
        ],
        compiler_params=pltpu.CompilerParams(
            collective_id=0, has_side_effects=True, vmem_limit_bytes=40 * 1024 * 1024),
    )(iterate)


def solution(mesh):
    return jax.shard_map(
        body, mesh=mesh,
        in_specs=(P(("layer", "panel"), "col"),),
        out_specs=P(("layer", "panel"), "col"),
        check_vma=False,
    )
```

```python
import jax
import jax.numpy as jnp
from jax import lax
from jax.experimental import pallas as pl
from jax.experimental.pallas import tpu as pltpu
from jax.sharding import PartitionSpec as P

NX, N, NLO = 4, 8, 4
HALF = N // 2
ROWS, COLS = 64, 512
PART = COLS // 2
MESH = pl.DeviceIdType.MESH
BF, F32 = jnp.bfloat16, jnp.float32


def kernel(x_ref, o_ref, ab, acc, gp, gr, g, gt, fp, fb, fh, fd, fs, f, first, sp, sb, sh, sd, ss, ow,
           ex_sem, a_sem, b_sem, gr_sem, g_sem, fr_sem, f_sem, sr_sem, out_sem):
    panel, col, layer = lax.axis_index("panel"), lax.axis_index("col"), lax.axis_index("layer")
    y, z_lo = panel // NLO, panel % NLO
    z_hi, x = col // NX, col % NX
    z = z_hi * NLO + z_lo
    o = 1 - layer

    def device(x, y, z):
        return (y * NLO + z % NLO, (z // NLO) * NX + x, layer)

    def place(zz):
        return (zz % NLO) * 2 + zz // NLO

    def ring_y(d):
        return device(x, (y + d + N) % N, z)

    def ring_z(d):
        return device(x, y, (z + d + N) % N)

    def ring1(d):
        return device(x, (y + o * d + N) % N, (z + (1 - o) * d + N) % N)

    def ring2(d):
        return device(x, (y + (1 - o) * d + N) % N, (z + o * d + N) % N)

    def place1(d):
        return (1 - o) * place((z + d + N) % N) + o * ((y + d + N) % N)

    def pos2(d):
        return ((1 - o) * y + o * z + d + N) % N

    def peer_x(d):
        return device((x + d) % NX, y, z)

    own1 = place1(0)
    partner = device(x, y, (z + HALF) % N)

    barrier = pltpu.get_barrier_semaphore()
    for d in range(1, N):
        pl.semaphore_signal(barrier, inc=1, device_id=ring_y(d), device_id_type=MESH)
        pl.semaphore_signal(barrier, inc=1, device_id=ring_z(d), device_id_type=MESH)
    for d in range(1, NX):
        pl.semaphore_signal(barrier, inc=1, device_id=peer_x(d), device_id_type=MESH)
    pl.semaphore_wait(barrier, 2 * (N - 1) + NX - 1)

    def remote(src, dst, send_sem, recv_sem, to):
        return pltpu.make_async_remote_copy(
            src_ref=src, dst_ref=dst, send_sem=send_sem, recv_sem=recv_sem, device_id=to, device_id_type=MESH)

    started = []

    def send(src, dst, send_sem, recv_sem, to):
        copy = remote(src, dst, send_sem, recv_sem, to)
        copy.start()
        started.append(copy)
        return copy

    def gather(slot, ring, sems, base, far):
        def one(code, src, d):
            return send(src, src, sems.at[0, base + code], sems.at[1, base + code], ring(d))

        own = slot(0)
        second = [one(0, own, 2), one(1, own, -2)]
        last = [one(2, own, 1), one(3, own, -1)]
        yield
        for way, sign in ((0, 1), (1, -1)):
            second[way].wait_recv()
            passed = slot(-2 * sign)
            part = far(way, passed)
            if part is not None:
                last.append(one(4 + way, part, 2 * sign))
            last.append(one(6 + way, passed, sign))
        yield
        for copy in last:
            copy.wait_recv()
        yield

    def scatter(parts, index, halves, relay, relay_half, direct, sums, ring, sems, base):
        def one(code, src, dst, d):
            return send(src, dst, sems.at[0, base + code], sems.at[1, base + code], ring(d))

        met, last = [], []
        for way, sign in ((0, -1), (1, 1)):
            met.append([one(way, parts.at[index(4 * sign)].at[halves[way]], relay_half.at[way], 2 * sign)])
        for way, sign in ((0, -1), (1, 1)):
            met[way].append(one(2 + way, parts.at[index(3 * sign)], relay.at[way], sign))
        for way, sign in ((0, -1), (1, 1)):
            last.append(one(4 + way, parts.at[index(sign)], direct.at[way], sign))
        yield
        for way, sign in ((0, -1), (1, 1)):
            for copy in met[way]:
                copy.wait_recv()
            sums[way] = (parts[index(2 * sign)].astype(F32) + relay[way].astype(F32)).astype(BF)
            half = halves[way]
            sums.at[way].at[half][...] = (parts.at[index(2 * sign)].at[half][...].astype(F32) + relay.at[way].at[half][...].astype(F32)
                                + relay_half[way].astype(F32)).astype(BF)
            last.append(one(6 + way, sums.at[way], direct.at[2 + way], 2 * sign))
        yield
        total = parts[index(0)].astype(F32)
        for i, copy in enumerate(last):
            copy.wait_recv()
            total += direct[i].astype(F32)
        yield total

    mine = pl.multiple_of(z_hi * ROWS, ROWS)
    other = pl.multiple_of((1 - z_hi) * ROWS, ROWS)

    exchange = send(x_ref.at[pl.ds(other, ROWS), :], ab.at[1 - o, z_hi, y], ex_sem.at[0, 0], ex_sem.at[1, 0], partner)

    def slot_a(u):
        def slot(d):
            zz = (z + d + N) % N
            return ab.at[o, zz // NLO, (zz % NLO) * 2 + u]
        return slot

    def slot_b(c):
        return lambda d: ab.at[1 - o, c, (y + d + N) % N]

    def one_way(u):
        return lambda way, ref: ref if way == u else None

    c_late = 1 - z_hi
    a0 = gather(slot_a(0), ring_z, a_sem, 0, one_way(0))
    a1 = gather(slot_a(1), ring_z, a_sem, 8, one_way(1))
    b0 = gather(slot_b(z_hi), ring_y, b_sem, 0, one_way(0))
    b1 = gather(slot_b(c_late), ring_y, b_sem, 8, one_way(1))
    ab[1 - o, z_hi, y] = x_ref[pl.ds(mine, ROWS), :]
    next(b0)
    for u in (0, 1):
        ab[o, z_hi, z_lo * 2 + u] = x_ref[u * ROWS:(u + 1) * ROWS, :]
    next(a0)
    next(a1)
    next(b0)
    next(a0)
    exchange.wait_recv()
    next(b1)
    next(a1)
    next(b1)
    next(b0)
    next(a0)
    next(a1)

    def nt(a, b):
        return lax.dot_general(a, b, (((1,), (1,)), ((), ())), preferred_element_type=F32)

    rows_all, rows_half = N * ROWS, HALF * ROWS
    acc[...] = nt(ab[0, z_hi].reshape(rows_all, COLS), ab[1, z_hi].reshape(rows_all, COLS))
    next(b1)

    gr_copies = []
    for k in (0, 1):
        block = acc[k * rows_half:(k + 1) * rows_half, :] + nt(
            ab[0, c_late, k * HALF:(k + 1) * HALF].reshape(rows_half, COLS), ab[1, c_late].reshape(rows_all, COLS))
        gp[k * HALF:(k + 1) * HALF] = block.astype(BF).reshape(HALF, ROWS, rows_all)
        gr_copies.append([
            send(gp.at[k * HALF + (x + d) % NX], gr.at[k, d - 1], gr_sem.at[0, k * 3 + d - 1],
                 gr_sem.at[1, k * 3 + d - 1], peer_x(d)) for d in (2, 1, 3)])
    g_copies = []
    for k in (0, 1):
        mine_g = k * HALF + x
        for c in gr_copies[k]:
            c.wait_recv()
        total = gp[mine_g].astype(F32)
        for d in range(NX - 1):
            total += gr[k, d].astype(F32)
        g[mine_g] = (total * (1.0 / 4096)).astype(BF)
        g_copies.append([
            send(g.at[mine_g], g.at[mine_g], g_sem.at[0, k * 3 + d - 1], g_sem.at[1, k * 3 + d - 1], peer_x(d))
            for d in (2, 1, 3)])

    row_halves = (pl.ds(0, ROWS // 2), pl.ds(ROWS // 2, ROWS // 2))
    firsts = [scatter(fp.at[v], place1, row_halves, fb.at[v], fh.at[v], fd.at[v], fs.at[v], ring1, fr_sem, v * 8)
              for v in (0, 1)]

    def part_of_first(k, v):
        rows = g[k * HALF:(k + 1) * HALF].reshape(rows_half, rows_all)
        for c in (0, 1):
            right = ab[1, c, :, :, v * PART:(v + 1) * PART].reshape(rows_all, PART)
            fp[v, k * HALF:(k + 1) * HALF, :, c * PART:(c + 1) * PART] = jnp.dot(
                rows, right, preferred_element_type=F32).astype(BF).reshape(HALF, ROWS, PART)

    for c in g_copies[0]:
        c.wait_recv()
    part_of_first(0, 0)
    for c in g_copies[1]:
        c.wait_recv()
    part_of_first(1, 0)
    next(firsts[0])
    part_of_first(0, 1)
    part_of_first(1, 1)
    next(firsts[1])
    gt[...] = g[...].reshape(rows_all, rows_all).T
    next(firsts[0])
    next(firsts[1])

    def both(way, ref):
        return ref.at[row_halves[way]]

    gathers = []
    for v in (0, 1):
        first[v] = next(firsts[v])
        f[v, own1] = first[v].astype(BF)
        gathers.append(gather(lambda d, v=v: f.at[v, place1(d)], ring1, f_sem, v * 8, both))
        next(gathers[v])
    next(gathers[0])
    next(gathers[1])

    seconds = [scatter(sp.at[v], pos2, (0, 1), sb.at[v], sh.at[v], sd.at[v], ss.at[v], ring2, sr_sem, v * 8)
               for v in (0, 1)]
    for v in (0, 1):
        next(gathers[v])
        second = 2.0315 * jnp.dot(gt[...], f[v].reshape(rows_all, COLS), preferred_element_type=F32)

        @pl.when(o == 0)
        def _():
            for t in range(N):
                for c in (0, 1):
                    part = second[t * ROWS:(t + 1) * ROWS, c * PART:(c + 1) * PART]
                    sp[v, t, c] = part.astype(BF)
            for c in (0, 1):
                sp[v, y, c] = (sp[v, y, c].astype(F32) - 4.775 * first[v, :, c * PART:(c + 1) * PART]).astype(BF)

        @pl.when(o == 1)
        def _():
            for t in range(N):
                for h in (0, 1):
                    at = ((t % NLO) * 2 + h) * ROWS
                    c = t // NLO
                    sp[v, t, h] = second[at:at + ROWS, c * PART:(c + 1) * PART].astype(BF)
            for c in (0, 1):
                at = c * NLO + z_lo
                sp[v, at, z_hi] = (
                    sp[v, at, z_hi].astype(F32) - 4.775 * first[v, :, c * PART:(c + 1) * PART]).astype(BF)

        next(seconds[v])
    next(seconds[0])
    for c in started[:-14]:
        c.wait_send()
    del started[:-14]
    next(seconds[1])

    def out_copy(v):
        return remote(ow.at[v, 1 - z_hi], o_ref.at[pl.ds(mine, ROWS), v * PART:(v + 1) * PART],
                      out_sem.at[0, v], out_sem.at[1, v], partner)

    for v in (0, 1):
        total = next(seconds[v])
        cols = slice(v * PART, (v + 1) * PART)

        @pl.when(o == 0)
        def _():
            for c in (0, 1):
                ow[v, c] = (3.4445 * ab[1, c, y, :, cols].astype(F32) + total[c]).astype(BF)
            out_copy(v).start()
            o_ref[pl.ds(mine, ROWS), cols] = ow[v, z_hi]

        @pl.when(o == 1)
        def _():
            for h in (0, 1):
                rows = slice(h * ROWS, (h + 1) * ROWS)
                o_ref[rows, cols] = (3.4445 * x_ref[rows, cols].astype(F32) + total[h]).astype(BF)

    for c in started:
        c.wait_send()

    @pl.when(o == 0)
    def _():
        for v in (0, 1):
            out_copy(v).wait()


def body(iterate):
    stack = pltpu.VMEM((2, N, ROWS, COLS), BF)
    gram = pltpu.VMEM((N, ROWS, N * ROWS), BF)
    chunks = lambda n: pltpu.VMEM((2, n, ROWS, COLS), BF)
    blocks = lambda n: pltpu.VMEM((2, n, 2, ROWS, PART), BF)
    dma = lambda n: pltpu.SemaphoreType.DMA((2, n))
    return pl.pallas_call(
        kernel,
        out_shape=jax.ShapeDtypeStruct(iterate.shape, BF),
        in_specs=[pl.BlockSpec(memory_space=pltpu.VMEM)],
        out_specs=pl.BlockSpec(memory_space=pltpu.VMEM),
        scratch_shapes=[
            pltpu.VMEM((2, 2, N, ROWS, COLS), BF),
            pltpu.VMEM((N * ROWS, N * ROWS), F32),
            gram, pltpu.VMEM((2, NX - 1, ROWS, N * ROWS), BF), gram,
            pltpu.VMEM((N * ROWS, N * ROWS), BF),
            stack,
            chunks(2), pltpu.VMEM((2, 2, ROWS // 2, COLS), BF), chunks(4), chunks(2),
            stack, pltpu.VMEM((2, ROWS, COLS), F32),
            blocks(N), blocks(2), pltpu.VMEM((2, 2, ROWS, PART), BF), blocks(4), blocks(2),
            pltpu.VMEM((2, 2, ROWS, PART), BF),
            dma(1), dma(16), dma(16), dma(6), dma(6), dma(16), dma(16), dma(16), dma(2),
        ],
        compiler_params=pltpu.CompilerParams(
            collective_id=0, has_side_effects=True, vmem_limit_bytes=40 * 1024 * 1024),
    )(iterate)


def solution(mesh):
    return jax.shard_map(
        body, mesh=mesh,
        in_specs=(P(("layer", "panel"), "col"),),
        out_specs=P(("layer", "panel"), "col"),
        check_vma=False,
    )
```

```python
import jax
import jax.numpy as jnp
from jax import lax
from jax.experimental import pallas as pl
from jax.experimental.pallas import tpu as pltpu
from jax.sharding import PartitionSpec as P

NX, N, NLO = 4, 8, 4
HALF = N // 2
ROWS, COLS = 64, 512
PART = COLS // 2
ORDER = ((4, 3, 5, 1), (7, 2, 6, 0))
SLOT = {d: k * 4 + i for k in (0, 1) for i, d in enumerate(ORDER[k])}
MESH = pl.DeviceIdType.MESH
BF, F32 = jnp.bfloat16, jnp.float32


def kernel(x_hbm, o_ref, x_ref, x_sem, ab, acc, gp, gr, g, gt, fp, fb, fh, fd, fs, f, first, sp, sb, sh, sd, ss, ow,
           ex_sem, a_sem, b_sem, gr_sem, g_sem, fr_sem, f_sem, sr_sem, out_sem):
    panel, col, layer = lax.axis_index("panel"), lax.axis_index("col"), lax.axis_index("layer")
    y, z_lo = panel // NLO, panel % NLO
    z_hi, x = col // NX, col % NX
    z = z_hi * NLO + z_lo
    o = 1 - layer

    def device(x, y, z):
        return (y * NLO + z % NLO, (z // NLO) * NX + x, layer)

    def place(zz):
        return (zz % NLO) * 2 + zz // NLO

    def ring_y(d):
        return device(x, (y + d + N) % N, z)

    def ring_z(d):
        return device(x, y, (z + d + N) % N)

    def ring1(d):
        return device(x, (y + o * d + N) % N, (z + (1 - o) * d + N) % N)

    def ring2(d):
        return device(x, (y + (1 - o) * d + N) % N, (z + o * d + N) % N)

    def place1(d):
        return (1 - o) * place((z + d + N) % N) + o * ((y + d + N) % N)

    def pos2(d):
        return ((1 - o) * y + o * z + d + N) % N

    def peer_x(d):
        return device((x + d) % NX, y, z)

    partner = device(x, y, (z + HALF) % N)

    barrier = pltpu.get_barrier_semaphore()
    greeted = [device(x, y, (z + HALF) % N)] + [ring(d) for d in (2, -2, 1, -1) for ring in (ring_z, ring_y)]
    greeted += [peer_x(d) for d in (2, 1, 3)]
    for peer in greeted:
        pl.semaphore_signal(barrier, inc=1, device_id=peer, device_id_type=MESH)
    load = pltpu.make_async_copy(x_hbm, x_ref, x_sem)
    load.start()
    pl.semaphore_wait(barrier, len(greeted))
    load.wait()

    def remote(src, dst, send_sem, recv_sem, to):
        return pltpu.make_async_remote_copy(
            src_ref=src, dst_ref=dst, send_sem=send_sem, recv_sem=recv_sem, device_id=to, device_id_type=MESH)

    started = []

    def send(src, dst, send_sem, recv_sem, to):
        copy = remote(src, dst, send_sem, recv_sem, to)
        copy.start()
        started.append(copy)
        return copy

    def gather(slot, ring, sems, base, far):
        def one(code, src, dst, d):
            return send(src, dst, sems.at[0, base + code], sems.at[1, base + code], ring(d))

        second = [one(0, slot(0, 0), slot(0, 2), 2), one(1, slot(0, 0), slot(0, -2), -2)]
        last = [one(2, slot(0, 0), slot(0, 1), 1), one(3, slot(0, 0), slot(0, -1), -1)]
        yield
        for way, sign in ((0, 1), (1, -1)):
            second[way].wait_recv()
            at = -2 * sign
            src, dst = far(way, slot(at, 0)), far(way, slot(at, 2 * sign))
            if src is not None:
                last.append(one(4 + way, src, dst, 2 * sign))
            last.append(one(6 + way, slot(at, 0), slot(at, sign), sign))
        yield
        for copy in last:
            copy.wait_recv()
        yield

    def scatter(parts, index, halves, relay, relay_half, direct, sums, ring, sems, base):
        def one(code, src, dst, d):
            return send(src, dst, sems.at[0, base + code], sems.at[1, base + code], ring(d))

        met, last = [], []
        for way, sign in ((0, -1), (1, 1)):
            met.append([one(way, parts.at[index(4 * sign)].at[halves[way]], relay_half.at[way], 2 * sign)])
        for way, sign in ((0, -1), (1, 1)):
            met[way].append(one(2 + way, parts.at[index(3 * sign)], relay.at[way], sign))
        for way, sign in ((1, 1), (0, -1)):
            last.append(one(4 + way, parts.at[index(sign)], direct.at[way], sign))
            yield
        for way, sign in ((0, -1), (1, 1)):
            for copy in met[way]:
                copy.wait_recv()
            sums[way] = (parts[index(2 * sign)].astype(F32) + relay[way].astype(F32)).astype(BF)
            half = halves[way]
            sums.at[way].at[half][...] = (parts.at[index(2 * sign)].at[half][...].astype(F32) + relay.at[way].at[half][...].astype(F32)
                                + relay_half[way].astype(F32)).astype(BF)
            last.append(one(6 + way, sums.at[way], direct.at[2 + way], 2 * sign))
        yield
        total = parts[index(0)].astype(F32)
        for i, copy in zip((1, 0, 2, 3), last):
            copy.wait_recv()
            total += direct[i].astype(F32)
        yield total

    mine = pl.multiple_of(z_hi * ROWS, ROWS)
    other = pl.multiple_of((1 - z_hi) * ROWS, ROWS)

    exchange = send(x_ref.at[pl.ds(other, ROWS), :], ab.at[1 - o, z_hi, y], ex_sem.at[0, 0], ex_sem.at[1, 0], partner)

    def slot_a(u):
        def slot(d, _):
            zz = (z + d + N) % N
            return ab.at[o, zz // NLO, (zz % NLO) * 2 + u]
        return slot

    def slot_b(c):
        return lambda d, _: ab.at[1 - o, c, (y + d + N) % N]

    row_halves = (pl.ds(0, ROWS // 2), pl.ds(ROWS // 2, ROWS // 2))

    def both(way, ref):
        return ref.at[row_halves[way]]

    c_late = 1 - z_hi
    a0 = gather(slot_a(0), ring_z, a_sem, 0, lambda way, ref: None)
    a1 = gather(slot_a(1), ring_z, a_sem, 8, lambda way, ref: None)
    b0 = gather(slot_b(z_hi), ring_y, b_sem, 0, both)
    b1 = gather(slot_b(c_late), ring_y, b_sem, 8, both)
    ab[1 - o, z_hi, y] = x_ref[pl.ds(mine, ROWS), :]
    next(b0)
    for u in (0, 1):
        ab[o, z_hi, z_lo * 2 + u] = x_ref[u * ROWS:(u + 1) * ROWS, :]
    next(a0)
    next(a1)
    next(b0)
    next(a0)
    exchange.wait_recv()
    next(b1)
    next(a1)
    far = []
    for way, sign in ((0, 1), (1, -1)):
        zz, unseen = (z - 2 * sign + N) % N, 1 - (z + 2 * sign + N) % N // NLO
        part = both(way, ab.at[o, zz // NLO, (zz % NLO) * 2 + unseen])
        far.append(send(part, part, a_sem.at[0, 4 + way], a_sem.at[1, 4 + way], ring_z(2 * sign)))
    ab[o, c_late, z_lo * 2 + z_hi] = ab[1 - o, c_late, y]
    next(b1)
    next(b0)
    next(a0)
    next(a1)
    for copy in far:
        copy.wait_recv()

    def nt(a, b):
        return lax.dot_general(a, b, (((1,), (1,)), ((), ())), preferred_element_type=F32)

    rows_all, rows_half = N * ROWS, HALF * ROWS
    def left(k, c):
        return jnp.concatenate([ab[0, c, place1(d)] for d in ORDER[k]], axis=0)

    for k in (0, 1):
        acc[k] = nt(left(k, z_hi), ab[1, z_hi].reshape(rows_all, COLS))
    next(b1)

    gr_copies = []
    for k in (0, 1):
        block = acc[k] + nt(left(k, c_late), ab[1, c_late].reshape(rows_all, COLS))
        gp[k * HALF:(k + 1) * HALF] = block.astype(BF).reshape(HALF, ROWS, rows_all)
        gr_copies.append([
            send(gp.at[k * HALF + (x + d) % NX], gr.at[k, d - 1], gr_sem.at[0, k * 3 + d - 1],
                 gr_sem.at[1, k * 3 + d - 1], peer_x(d)) for d in (2, 1, 3)])
    g_copies = []
    for k in (0, 1):
        mine_g = k * HALF + x
        for c in gr_copies[k]:
            c.wait_recv()
        total = gp[mine_g].astype(F32)
        for d in range(NX - 1):
            total += gr[k, d].astype(F32)
        g[mine_g] = (total * (1.0 / 4096)).astype(BF)
        g_copies.append([
            send(g.at[mine_g], g.at[mine_g], g_sem.at[0, k * 3 + d - 1], g_sem.at[1, k * 3 + d - 1], peer_x(d))
            for d in (2, 1, 3)])

    firsts = [scatter(fp.at[v], lambda d: SLOT[d % N], row_halves, fb.at[v], fh.at[v], fd.at[v], fs.at[v], ring1, fr_sem, v * 8)
              for v in (0, 1)]

    def part_of_first(k, v):
        rows = g[k * HALF:(k + 1) * HALF].reshape(rows_half, rows_all)
        for c in (0, 1):
            right = ab[1, c, :, :, v * PART:(v + 1) * PART].reshape(rows_all, PART)
            fp[v, k * HALF:(k + 1) * HALF, :, c * PART:(c + 1) * PART] = jnp.dot(
                rows, right, preferred_element_type=F32).astype(BF).reshape(HALF, ROWS, PART)

    for k in (0, 1):
        for c in g_copies[k]:
            c.wait_recv()
        for v in (0, 1):
            part_of_first(k, v)
            next(firsts[v])
    gt[...] = g[...].reshape(rows_all, rows_all).T
    next(firsts[0])
    next(firsts[1])

    gathers = []
    for v in (0, 1):
        first[v] = next(firsts[v])
        f[v, SLOT[0]] = first[v].astype(BF)
        gathers.append(gather(lambda d, to, v=v: f.at[v, SLOT[(d - to) % N]], ring1, f_sem, v * 8, both))
        next(gathers[v])
    next(gathers[0])
    next(gathers[1])

    seconds = [scatter(sp.at[v], pos2, (0, 1), sb.at[v], sh.at[v], sd.at[v], ss.at[v], ring2, sr_sem, v * 8)
               for v in (0, 1)]
    for v in (0, 1):
        next(gathers[v])
        second = 2.0315 * jnp.dot(gt[...], f[v].reshape(rows_all, COLS), preferred_element_type=F32)

        @pl.when(o == 0)
        def _():
            for t in range(N):
                for c in (0, 1):
                    part = second[t * ROWS:(t + 1) * ROWS, c * PART:(c + 1) * PART]
                    sp[v, t, c] = part.astype(BF)
            for c in (0, 1):
                sp[v, y, c] = (sp[v, y, c].astype(F32) - 4.775 * first[v, :, c * PART:(c + 1) * PART]).astype(BF)

        @pl.when(o == 1)
        def _():
            for t in range(N):
                for h in (0, 1):
                    at = ((t % NLO) * 2 + h) * ROWS
                    c = t // NLO
                    sp[v, t, h] = second[at:at + ROWS, c * PART:(c + 1) * PART].astype(BF)
            for c in (0, 1):
                at = c * NLO + z_lo
                sp[v, at, z_hi] = (
                    sp[v, at, z_hi].astype(F32) - 4.775 * first[v, :, c * PART:(c + 1) * PART]).astype(BF)

        next(seconds[v])
        next(seconds[v])
    next(seconds[0])
    for c in started[:-14]:
        c.wait_send()
    del started[:-14]
    next(seconds[1])

    def out_copy(v):
        return remote(ow.at[v, 1 - z_hi], o_ref.at[pl.ds(mine, ROWS), v * PART:(v + 1) * PART],
                      out_sem.at[0, v], out_sem.at[1, v], partner)

    for v in (0, 1):
        total = next(seconds[v])
        cols = slice(v * PART, (v + 1) * PART)

        @pl.when(o == 0)
        def _():
            for c in (0, 1):
                ow[v, c] = (3.4445 * ab[1, c, y, :, cols].astype(F32) + total[c]).astype(BF)
            out_copy(v).start()
            o_ref[pl.ds(mine, ROWS), cols] = ow[v, z_hi]

        @pl.when(o == 1)
        def _():
            for h in (0, 1):
                rows = slice(h * ROWS, (h + 1) * ROWS)
                o_ref[rows, cols] = (3.4445 * x_ref[rows, cols].astype(F32) + total[h]).astype(BF)

    for c in started:
        c.wait_send()

    @pl.when(o == 0)
    def _():
        for v in (0, 1):
            out_copy(v).wait()


def body(iterate):
    stack = pltpu.VMEM((2, N, ROWS, COLS), BF)
    gram = pltpu.VMEM((N, ROWS, N * ROWS), BF)
    chunks = lambda n: pltpu.VMEM((2, n, ROWS, COLS), BF)
    blocks = lambda n: pltpu.VMEM((2, n, 2, ROWS, PART), BF)
    dma = lambda n: pltpu.SemaphoreType.DMA((2, n))
    return pl.pallas_call(
        kernel,
        out_shape=jax.ShapeDtypeStruct(iterate.shape, BF),
        in_specs=[pl.BlockSpec(memory_space=pl.ANY)],
        out_specs=pl.BlockSpec(memory_space=pltpu.VMEM),
        scratch_shapes=[
            pltpu.VMEM(iterate.shape, BF), pltpu.SemaphoreType.DMA(()),
            pltpu.VMEM((2, 2, N, ROWS, COLS), BF),
            pltpu.VMEM((2, HALF * ROWS, N * ROWS), F32),
            gram, pltpu.VMEM((2, NX - 1, ROWS, N * ROWS), BF), gram,
            pltpu.VMEM((N * ROWS, N * ROWS), BF),
            stack,
            chunks(2), pltpu.VMEM((2, 2, ROWS // 2, COLS), BF), chunks(4), chunks(2),
            stack, pltpu.VMEM((2, ROWS, COLS), F32),
            blocks(N), blocks(2), pltpu.VMEM((2, 2, ROWS, PART), BF), blocks(4), blocks(2),
            pltpu.VMEM((2, 2, ROWS, PART), BF),
            dma(1), dma(16), dma(16), dma(6), dma(6), dma(16), dma(16), dma(16), dma(2),
        ],
        compiler_params=pltpu.CompilerParams(
            collective_id=0, has_side_effects=True, vmem_limit_bytes=40 * 1024 * 1024),
    )(iterate)


def solution(mesh):
    return jax.shard_map(
        body, mesh=mesh,
        in_specs=(P(("layer", "panel"), "col"),),
        out_specs=P(("layer", "panel"), "col"),
        check_vma=False,
    )
```

```python
import jax
import jax.numpy as jnp
from jax import lax
from jax.experimental import pallas as pl
from jax.experimental.pallas import tpu as pltpu
from jax.sharding import PartitionSpec as P

NX, N, NLO = 4, 8, 4
HALF = N // 2
ROWS, COLS = 64, 512
PIECES = 4
PART = COLS // PIECES
ORDER = ((4, 3, 5, 1), (7, 2, 6, 0))
SLOT = {d: k * 4 + i for k in (0, 1) for i, d in enumerate(ORDER[k])}
MESH = pl.DeviceIdType.MESH
BF, F32 = jnp.bfloat16, jnp.float32


def kernel(x_hbm, o_ref, x_ref, x_sem, ab, acc, gp, gr, g, gt, fp, fb, fh, fd, fs, f, first, sp, sb, sh, sd, ss, ow,
           ex_sem, a_sem, b_sem, gr_sem, g_sem, fr_sem, f_sem, sr_sem, out_sem):
    panel, col, layer = lax.axis_index("panel"), lax.axis_index("col"), lax.axis_index("layer")
    y, z_lo = panel // NLO, panel % NLO
    z_hi, x = col // NX, col % NX
    z = z_hi * NLO + z_lo
    o = 1 - layer

    def device(x, y, z):
        return (y * NLO + z % NLO, (z // NLO) * NX + x, layer)

    def place(zz):
        return (zz % NLO) * 2 + zz // NLO

    def ring_y(d):
        return device(x, (y + d + N) % N, z)

    def ring_z(d):
        return device(x, y, (z + d + N) % N)

    def ring1(d):
        return device(x, (y + o * d + N) % N, (z + (1 - o) * d + N) % N)

    def ring2(d):
        return device(x, (y + (1 - o) * d + N) % N, (z + o * d + N) % N)

    def place1(d):
        return (1 - o) * place((z + d + N) % N) + o * ((y + d + N) % N)

    def pos2(d):
        return ((1 - o) * y + o * z + d + N) % N

    def peer_x(d):
        return device((x + d) % NX, y, z)

    partner = device(x, y, (z + HALF) % N)

    barrier = pltpu.get_barrier_semaphore()
    greeted = [device(x, y, (z + HALF) % N)] + [ring(d) for d in (2, -2, 1, -1) for ring in (ring_z, ring_y)]
    greeted += [peer_x(d) for d in (2, 1, 3)]
    for peer in greeted:
        pl.semaphore_signal(barrier, inc=1, device_id=peer, device_id_type=MESH)
    load = pltpu.make_async_copy(x_hbm, x_ref, x_sem)
    load.start()
    pl.semaphore_wait(barrier, len(greeted))
    load.wait()

    def remote(src, dst, send_sem, recv_sem, to):
        return pltpu.make_async_remote_copy(
            src_ref=src, dst_ref=dst, send_sem=send_sem, recv_sem=recv_sem, device_id=to, device_id_type=MESH)

    started = []

    def send(src, dst, send_sem, recv_sem, to):
        copy = remote(src, dst, send_sem, recv_sem, to)
        copy.start()
        started.append(copy)
        return copy

    def gather(slot, ring, sems, base, far):
        def one(code, src, dst, d):
            return send(src, dst, sems.at[0, base + code], sems.at[1, base + code], ring(d))

        second = [one(0, slot(0, 0), slot(0, 2), 2), one(1, slot(0, 0), slot(0, -2), -2)]
        last = [one(2, slot(0, 0), slot(0, 1), 1), one(3, slot(0, 0), slot(0, -1), -1)]
        yield
        for way, sign in ((0, 1), (1, -1)):
            second[way].wait_recv()
            at = -2 * sign
            src, dst = far(way, slot(at, 0)), far(way, slot(at, 2 * sign))
            if src is not None:
                last.append(one(4 + way, src, dst, 2 * sign))
            last.append(one(6 + way, slot(at, 0), slot(at, sign), sign))
        yield
        for copy in last:
            copy.wait_recv()
        yield

    def scatter(parts, index, halves, relay, relay_half, direct, sums, ring, sems, base):
        def one(code, src, dst, d):
            return send(src, dst, sems.at[0, base + code], sems.at[1, base + code], ring(d))

        met, last = [], []
        for way, sign in ((0, -1), (1, 1)):
            met.append([one(way, parts.at[index(4 * sign)].at[halves[way]], relay_half.at[way], 2 * sign)])
        for way, sign in ((0, -1), (1, 1)):
            met[way].append(one(2 + way, parts.at[index(3 * sign)], relay.at[way], sign))
        for way, sign in ((1, 1), (0, -1)):
            last.append(one(4 + way, parts.at[index(sign)], direct.at[way], sign))
            yield
        for way, sign in ((0, -1), (1, 1)):
            for copy in met[way]:
                copy.wait_recv()
            sums[way] = (parts[index(2 * sign)].astype(F32) + relay[way].astype(F32)).astype(BF)
            half = halves[way]
            sums.at[way].at[half][...] = (parts.at[index(2 * sign)].at[half][...].astype(F32) + relay.at[way].at[half][...].astype(F32)
                                + relay_half[way].astype(F32)).astype(BF)
            last.append(one(6 + way, sums.at[way], direct.at[2 + way], 2 * sign))
        yield
        total = parts[index(0)].astype(F32)
        for i, copy in zip((1, 0, 2, 3), last):
            copy.wait_recv()
            total += direct[i].astype(F32)
        yield total

    mine = pl.multiple_of(z_hi * ROWS, ROWS)
    other = pl.multiple_of((1 - z_hi) * ROWS, ROWS)

    exchange = send(x_ref.at[pl.ds(other, ROWS), :], ab.at[1 - o, z_hi, y], ex_sem.at[0, 0], ex_sem.at[1, 0], partner)

    def slot_a(u):
        def slot(d, _):
            zz = (z + d + N) % N
            return ab.at[o, zz // NLO, (zz % NLO) * 2 + u]
        return slot

    def slot_b(c):
        return lambda d, _: ab.at[1 - o, c, (y + d + N) % N]

    row_halves = (pl.ds(0, ROWS // 2), pl.ds(ROWS // 2, ROWS // 2))

    def both(way, ref):
        return ref.at[row_halves[way]]

    c_late = 1 - z_hi
    a0 = gather(slot_a(0), ring_z, a_sem, 0, lambda way, ref: None)
    a1 = gather(slot_a(1), ring_z, a_sem, 8, lambda way, ref: None)
    b0 = gather(slot_b(z_hi), ring_y, b_sem, 0, both)
    b1 = gather(slot_b(c_late), ring_y, b_sem, 8, both)
    ab[1 - o, z_hi, y] = x_ref[pl.ds(mine, ROWS), :]
    next(b0)
    for u in (0, 1):
        ab[o, z_hi, z_lo * 2 + u] = x_ref[u * ROWS:(u + 1) * ROWS, :]
    next(a0)
    next(a1)
    next(b0)
    exchange.wait_recv()
    next(b1)
    next(a0)
    next(a1)
    far = []
    for way, sign in ((0, 1), (1, -1)):
        zz, unseen = (z - 2 * sign + N) % N, 1 - (z + 2 * sign + N) % N // NLO
        part = both(way, ab.at[o, zz // NLO, (zz % NLO) * 2 + unseen])
        far.append(send(part, part, a_sem.at[0, 4 + way], a_sem.at[1, 4 + way], ring_z(2 * sign)))
    ab[o, c_late, z_lo * 2 + z_hi] = ab[1 - o, c_late, y]
    next(b1)
    next(b0)
    next(a0)
    next(a1)
    for copy in far:
        copy.wait_recv()

    def nt(a, b):
        return lax.dot_general(a, b, (((1,), (1,)), ((), ())), preferred_element_type=F32)

    rows_all, rows_half = N * ROWS, HALF * ROWS
    def left(k, c):
        return jnp.concatenate([ab[0, c, place1(d)] for d in ORDER[k]], axis=0)

    for k in (0, 1):
        acc[k] = nt(left(k, z_hi), ab[1, z_hi].reshape(rows_all, COLS))
    next(b1)

    gr_copies = []
    for k in (0, 1):
        block = acc[k] + nt(left(k, c_late), ab[1, c_late].reshape(rows_all, COLS))
        gp[k * HALF:(k + 1) * HALF] = block.astype(BF).reshape(HALF, ROWS, rows_all)
        gr_copies.append([
            send(gp.at[k * HALF + (x + d) % NX], gr.at[k, d - 1], gr_sem.at[0, k * 3 + d - 1],
                 gr_sem.at[1, k * 3 + d - 1], peer_x(d)) for d in (2, 1, 3)])
    g_copies = []
    for k in (0, 1):
        mine_g = k * HALF + x
        for c in gr_copies[k]:
            c.wait_recv()
        total = gp[mine_g].astype(F32)
        for d in range(NX - 1):
            total += gr[k, d].astype(F32)
        g[mine_g] = (total * (1.0 / 4096)).astype(BF)
        g_copies.append([
            send(g.at[mine_g], g.at[mine_g], g_sem.at[0, k * 3 + d - 1], g_sem.at[1, k * 3 + d - 1], peer_x(d))
            for d in (2, 1, 3)])

    firsts = [scatter(fp.at[v], lambda d: SLOT[d % N], row_halves, fb.at[v], fh.at[v], fd.at[v], fs.at[v], ring1, fr_sem, v * 8)
              for v in range(PIECES)]

    def part_of_first(k, v):
        rows = g[k * HALF:(k + 1) * HALF].reshape(rows_half, rows_all)
        for c in (0, 1):
            right = ab[1, c, :, :, v * PART:(v + 1) * PART].reshape(rows_all, PART)
            fp[v, k * HALF:(k + 1) * HALF, :, c * PART:(c + 1) * PART] = jnp.dot(
                rows, right, preferred_element_type=F32).astype(BF).reshape(HALF, ROWS, PART)

    for k in (0, 1):
        for c in g_copies[k]:
            c.wait_recv()
        for v in range(PIECES):
            part_of_first(k, v)
            next(firsts[v])
    gt[...] = g[...].reshape(rows_all, rows_all).T
    for v in range(PIECES):
        next(firsts[v])


    gathers = []
    for v in range(PIECES):
        first[v] = next(firsts[v])
        f[v, SLOT[0]] = first[v].astype(BF)
        gathers.append(gather(lambda d, to, v=v: f.at[v, SLOT[(d - to) % N]], ring1, f_sem, v * 8, both))
        next(gathers[v])
    for v in range(PIECES):
        next(gathers[v])


    seconds = [scatter(sp.at[v], pos2, (0, 1), sb.at[v], sh.at[v], sd.at[v], ss.at[v], ring2, sr_sem, v * 8)
               for v in range(PIECES)]
    for v in range(PIECES):
        next(gathers[v])
        second = 2.0315 * jnp.dot(gt[...], f[v].reshape(rows_all, 2 * PART), preferred_element_type=F32)

        @pl.when(o == 0)
        def _():
            for t in range(N):
                for c in (0, 1):
                    part = second[t * ROWS:(t + 1) * ROWS, c * PART:(c + 1) * PART]
                    sp[v, t, c] = part.astype(BF)
            for c in (0, 1):
                sp[v, y, c] = (sp[v, y, c].astype(F32) - 4.775 * first[v, :, c * PART:(c + 1) * PART]).astype(BF)

        @pl.when(o == 1)
        def _():
            for t in range(N):
                for h in (0, 1):
                    at = ((t % NLO) * 2 + h) * ROWS
                    c = t // NLO
                    sp[v, t, h] = second[at:at + ROWS, c * PART:(c + 1) * PART].astype(BF)
            for c in (0, 1):
                at = c * NLO + z_lo
                sp[v, at, z_hi] = (
                    sp[v, at, z_hi].astype(F32) - 4.775 * first[v, :, c * PART:(c + 1) * PART]).astype(BF)

        next(seconds[v])
        next(seconds[v])
    for v in range(PIECES):
        next(seconds[v])

    for c in started[:-2 * PIECES]:
        c.wait_send()
    del started[:-2 * PIECES]

    def out_copy(v):
        return remote(ow.at[v, 1 - z_hi], o_ref.at[pl.ds(mine, ROWS), v * PART:(v + 1) * PART],
                      out_sem.at[0, v], out_sem.at[1, v], partner)

    for v in range(PIECES):
        total = next(seconds[v])
        cols = slice(v * PART, (v + 1) * PART)

        @pl.when(o == 0)
        def _():
            for c in (0, 1):
                ow[v, c] = (3.4445 * ab[1, c, y, :, cols].astype(F32) + total[c]).astype(BF)
            out_copy(v).start()
            o_ref[pl.ds(mine, ROWS), cols] = ow[v, z_hi]

        @pl.when(o == 1)
        def _():
            for h in (0, 1):
                rows = slice(h * ROWS, (h + 1) * ROWS)
                o_ref[rows, cols] = (3.4445 * x_ref[rows, cols].astype(F32) + total[h]).astype(BF)

    for c in started:
        c.wait_send()

    @pl.when(o == 0)
    def _():
        for v in range(PIECES):
            out_copy(v).wait()


def body(iterate):
    stack = pltpu.VMEM((PIECES, N, ROWS, 2 * PART), BF)
    gram = pltpu.VMEM((N, ROWS, N * ROWS), BF)
    chunks = lambda n: pltpu.VMEM((PIECES, n, ROWS, 2 * PART), BF)
    blocks = lambda n: pltpu.VMEM((PIECES, n, 2, ROWS, PART), BF)
    dma = lambda n: pltpu.SemaphoreType.DMA((2, n))
    return pl.pallas_call(
        kernel,
        out_shape=jax.ShapeDtypeStruct(iterate.shape, BF),
        in_specs=[pl.BlockSpec(memory_space=pl.ANY)],
        out_specs=pl.BlockSpec(memory_space=pltpu.VMEM),
        scratch_shapes=[
            pltpu.VMEM(iterate.shape, BF), pltpu.SemaphoreType.DMA(()),
            pltpu.VMEM((2, 2, N, ROWS, COLS), BF),
            pltpu.VMEM((2, HALF * ROWS, N * ROWS), F32),
            gram, pltpu.VMEM((2, NX - 1, ROWS, N * ROWS), BF), gram,
            pltpu.VMEM((N * ROWS, N * ROWS), BF),
            stack,
            chunks(2), pltpu.VMEM((PIECES, 2, ROWS // 2, 2 * PART), BF), chunks(4), chunks(2),
            stack, pltpu.VMEM((PIECES, ROWS, 2 * PART), F32),
            blocks(N), blocks(2), pltpu.VMEM((PIECES, 2, ROWS, PART), BF), blocks(4), blocks(2),
            pltpu.VMEM((PIECES, 2, ROWS, PART), BF),
            dma(1), dma(16), dma(16), dma(6), dma(6), dma(8 * PIECES), dma(8 * PIECES), dma(8 * PIECES), dma(PIECES),
        ],
        compiler_params=pltpu.CompilerParams(
            collective_id=0, has_side_effects=True, vmem_limit_bytes=40 * 1024 * 1024),
    )(iterate)


def solution(mesh):
    return jax.shard_map(
        body, mesh=mesh,
        in_specs=(P(("layer", "panel"), "col"),),
        out_specs=P(("layer", "panel"), "col"),
        check_vma=False,
    )
```

```python
import jax
import jax.numpy as jnp
from jax import lax
from jax.experimental import pallas as pl
from jax.experimental.pallas import tpu as pltpu
from jax.sharding import PartitionSpec as P

NX, N, NLO = 4, 8, 4
HALF = N // 2
ROWS, COLS = 64, 512
PIECES = 4
PART = COLS // PIECES
ORDER = ((4, 3, 5, 1), (7, 2, 6, 0))
SLOT = {d: k * 4 + i for k in (0, 1) for i, d in enumerate(ORDER[k])}
MESH = pl.DeviceIdType.MESH
BF, F32 = jnp.bfloat16, jnp.float32


def kernel(x_hbm, o_ref, x_ref, x_sem, ab, acc, gp, gr, g, gt, fp, fb, fh, fd, fs, f, first, sp, sb, sh, sd, ss, ow,
           ex_sem, a_sem, b_sem, gr_sem, g_sem, fr_sem, f_sem, sr_sem, out_sem):
    panel, col, layer = lax.axis_index("panel"), lax.axis_index("col"), lax.axis_index("layer")
    y, z_lo = panel // NLO, panel % NLO
    z_hi, x = col // NX, col % NX
    z = z_hi * NLO + z_lo
    o = 1 - layer

    def device(x, y, z):
        return (y * NLO + z % NLO, (z // NLO) * NX + x, layer)

    def place(zz):
        return (zz % NLO) * 2 + zz // NLO

    def ring_y(d):
        return device(x, (y + d + N) % N, z)

    def ring_z(d):
        return device(x, y, (z + d + N) % N)

    def ring1(d):
        return device(x, (y + o * d + N) % N, (z + (1 - o) * d + N) % N)

    def ring2(d):
        return device(x, (y + (1 - o) * d + N) % N, (z + o * d + N) % N)

    def place1(d):
        return (1 - o) * place((z + d + N) % N) + o * ((y + d + N) % N)

    def pos2(d):
        return ((1 - o) * y + o * z + d + N) % N

    def peer_x(d):
        return device((x + d) % NX, y, z)

    partner = device(x, y, (z + HALF) % N)

    barrier = pltpu.get_barrier_semaphore()
    greeted = [device(x, y, (z + HALF) % N)] + [ring(d) for d in (2, -2, 1, -1) for ring in (ring_z, ring_y)]
    greeted += [peer_x(d) for d in (2, 1, 3)]
    for peer in greeted:
        pl.semaphore_signal(barrier, inc=1, device_id=peer, device_id_type=MESH)
    load = pltpu.make_async_copy(x_hbm, x_ref, x_sem)
    load.start()
    pl.semaphore_wait(barrier, len(greeted))
    load.wait()

    def remote(src, dst, send_sem, recv_sem, to):
        return pltpu.make_async_remote_copy(
            src_ref=src, dst_ref=dst, send_sem=send_sem, recv_sem=recv_sem, device_id=to, device_id_type=MESH)

    started = []

    def send(src, dst, send_sem, recv_sem, to):
        copy = remote(src, dst, send_sem, recv_sem, to)
        copy.start()
        started.append(copy)
        return copy

    def gather(slot, ring, sems, base, far):
        def one(code, src, dst, d):
            return send(src, dst, sems.at[0, base + code], sems.at[1, base + code], ring(d))

        second = [one(0, slot(0, 0), slot(0, 2), 2), one(1, slot(0, 0), slot(0, -2), -2)]
        last = [one(2, slot(0, 0), slot(0, 1), 1), one(3, slot(0, 0), slot(0, -1), -1)]
        yield
        for way, sign in ((0, 1), (1, -1)):
            second[way].wait_recv()
            at = -2 * sign
            src, dst = far(way, slot(at, 0)), far(way, slot(at, 2 * sign))
            if src is not None:
                last.append(one(4 + way, src, dst, 2 * sign))
            last.append(one(6 + way, slot(at, 0), slot(at, sign), sign))
        yield
        for copy in last:
            copy.wait_recv()
        yield

    def scatter(parts, index, halves, relay, relay_half, direct, sums, ring, sems, base):
        def one(code, src, dst, d):
            return send(src, dst, sems.at[0, base + code], sems.at[1, base + code], ring(d))

        met, last = [], []
        for way, sign in ((0, -1), (1, 1)):
            met.append([one(way, parts.at[index(4 * sign)].at[halves[way]], relay_half.at[way], 2 * sign)])
        for way, sign in ((0, -1), (1, 1)):
            met[way].append(one(2 + way, parts.at[index(3 * sign)], relay.at[way], sign))
        for way, sign in ((1, 1), (0, -1)):
            last.append(one(4 + way, parts.at[index(sign)], direct.at[way], sign))
            yield
        for way, sign in ((0, -1), (1, 1)):
            for copy in met[way]:
                copy.wait_recv()
            sums[way] = (parts[index(2 * sign)].astype(F32) + relay[way].astype(F32)).astype(BF)
            half = halves[way]
            sums.at[way].at[half][...] = (parts.at[index(2 * sign)].at[half][...].astype(F32) + relay.at[way].at[half][...].astype(F32)
                                + relay_half[way].astype(F32)).astype(BF)
            last.append(one(6 + way, sums.at[way], direct.at[2 + way], 2 * sign))
        yield
        total = parts[index(0)].astype(F32)
        for i, copy in zip((1, 0, 2, 3), last):
            copy.wait_recv()
            total += direct[i].astype(F32)
        yield total

    mine = pl.multiple_of(z_hi * ROWS, ROWS)
    other = pl.multiple_of((1 - z_hi) * ROWS, ROWS)

    exchange = send(x_ref.at[pl.ds(other, ROWS), :], ab.at[1 - o, z_hi, y], ex_sem.at[0, 0], ex_sem.at[1, 0], partner)

    def slot_a(u):
        def slot(d, _):
            zz = (z + d + N) % N
            return ab.at[o, zz // NLO, (zz % NLO) * 2 + u]
        return slot

    def slot_b(c):
        return lambda d, _: ab.at[1 - o, c, (y + d + N) % N]

    row_halves = (pl.ds(0, ROWS // 2), pl.ds(ROWS // 2, ROWS // 2))

    def both(way, ref):
        return ref.at[row_halves[way]]

    c_late = 1 - z_hi
    a0 = gather(slot_a(0), ring_z, a_sem, 0, lambda way, ref: None)
    a1 = gather(slot_a(1), ring_z, a_sem, 8, lambda way, ref: None)
    b0 = gather(slot_b(z_hi), ring_y, b_sem, 0, both)
    b1 = gather(slot_b(c_late), ring_y, b_sem, 8, both)
    ab[1 - o, z_hi, y] = x_ref[pl.ds(mine, ROWS), :]
    next(b0)
    for u in (0, 1):
        ab[o, z_hi, z_lo * 2 + u] = x_ref[u * ROWS:(u + 1) * ROWS, :]
    next(a0)
    next(a1)
    next(b0)
    exchange.wait_recv()
    next(b1)
    next(a0)
    next(a1)
    far = []
    for way, sign in ((0, 1), (1, -1)):
        zz, unseen = (z - 2 * sign + N) % N, 1 - (z + 2 * sign + N) % N // NLO
        part = both(way, ab.at[o, zz // NLO, (zz % NLO) * 2 + unseen])
        far.append(send(part, part, a_sem.at[0, 4 + way], a_sem.at[1, 4 + way], ring_z(2 * sign)))
    ab[o, c_late, z_lo * 2 + z_hi] = ab[1 - o, c_late, y]
    next(b1)
    next(b0)
    next(a0)
    next(a1)
    for copy in far:
        copy.wait_recv()

    def nt(a, b):
        return lax.dot_general(a, b, (((1,), (1,)), ((), ())), preferred_element_type=F32)

    rows_all, rows_half = N * ROWS, HALF * ROWS
    def left(k, c):
        return jnp.concatenate([ab[0, c, place1(d)] for d in ORDER[k]], axis=0)

    for k in (0, 1):
        acc[k] = nt(left(k, z_hi), ab[1, z_hi].reshape(rows_all, COLS))
    next(b1)

    gr_copies = []
    for k in (0, 1):
        block = acc[k] + nt(left(k, c_late), ab[1, c_late].reshape(rows_all, COLS))
        gp[k * HALF:(k + 1) * HALF] = block.astype(BF).reshape(HALF, ROWS, rows_all)
        gr_copies.append([
            send(gp.at[k * HALF + (x + d) % NX], gr.at[k, d - 1], gr_sem.at[0, k * 3 + d - 1],
                 gr_sem.at[1, k * 3 + d - 1], peer_x(d)) for d in (2, 1, 3)])
    g_copies = []
    for k in (0, 1):
        mine_g = k * HALF + x
        for c in gr_copies[k]:
            c.wait_recv()
        total = gp[mine_g].astype(F32)
        for d in range(NX - 1):
            total += gr[k, d].astype(F32)
        g[mine_g] = (total * (1.0 / 4096)).astype(BF)
        g_copies.append([
            send(g.at[mine_g], g.at[mine_g], g_sem.at[0, k * 3 + d - 1], g_sem.at[1, k * 3 + d - 1], peer_x(d))
            for d in (2, 1, 3)])

    firsts = [scatter(fp.at[v], lambda d: SLOT[d % N], row_halves, fb.at[v], fh.at[v], fd.at[v], fs.at[v], ring1, fr_sem, v * 8)
              for v in range(PIECES)]

    def part_of_first(k, v):
        rows = g[k * HALF:(k + 1) * HALF].reshape(rows_half, rows_all)
        for c in (0, 1):
            right = ab[1, c, :, :, v * PART:(v + 1) * PART].reshape(rows_all, PART)
            fp[v, k * HALF:(k + 1) * HALF, :, c * PART:(c + 1) * PART] = jnp.dot(
                rows, right, preferred_element_type=F32).astype(BF).reshape(HALF, ROWS, PART)

    for k in (0, 1):
        for c in g_copies[k]:
            c.wait_recv()
        for v in range(PIECES):
            part_of_first(k, v)
            next(firsts[v])
            if k == 1:
                next(firsts[v])
    gt[...] = g[...].reshape(rows_all, rows_all).T


    gathers = []
    for v in range(PIECES):
        first[v] = next(firsts[v])
        f[v, SLOT[0]] = first[v].astype(BF)
        gathers.append(gather(lambda d, to, v=v: f.at[v, SLOT[(d - to) % N]], ring1, f_sem, v * 8, both))
        next(gathers[v])
    for v in range(PIECES):
        next(gathers[v])


    seconds = [scatter(sp.at[v], pos2, (0, 1), sb.at[v], sh.at[v], sd.at[v], ss.at[v], ring2, sr_sem, v * 8)
               for v in range(PIECES)]
    for v in range(PIECES):
        next(gathers[v])
        second = 2.0315 * jnp.dot(gt[...], f[v].reshape(rows_all, 2 * PART), preferred_element_type=F32)

        @pl.when(o == 0)
        def _():
            for t in range(N):
                for c in (0, 1):
                    part = second[t * ROWS:(t + 1) * ROWS, c * PART:(c + 1) * PART]
                    sp[v, t, c] = part.astype(BF)
            for c in (0, 1):
                sp[v, y, c] = (sp[v, y, c].astype(F32) - 4.775 * first[v, :, c * PART:(c + 1) * PART]).astype(BF)

        @pl.when(o == 1)
        def _():
            for t in range(N):
                for h in (0, 1):
                    at = ((t % NLO) * 2 + h) * ROWS
                    c = t // NLO
                    sp[v, t, h] = second[at:at + ROWS, c * PART:(c + 1) * PART].astype(BF)
            for c in (0, 1):
                at = c * NLO + z_lo
                sp[v, at, z_hi] = (
                    sp[v, at, z_hi].astype(F32) - 4.775 * first[v, :, c * PART:(c + 1) * PART]).astype(BF)

        next(seconds[v])
        next(seconds[v])
    for v in range(PIECES):
        next(seconds[v])

    for c in started[:-2 * PIECES]:
        c.wait_send()
    del started[:-2 * PIECES]

    def out_copy(v):
        return remote(ow.at[v, 1 - z_hi], o_ref.at[pl.ds(mine, ROWS), v * PART:(v + 1) * PART],
                      out_sem.at[0, v], out_sem.at[1, v], partner)

    for v in range(PIECES):
        total = next(seconds[v])
        cols = slice(v * PART, (v + 1) * PART)

        @pl.when(o == 0)
        def _():
            for c in (0, 1):
                ow[v, c] = (3.4445 * ab[1, c, y, :, cols].astype(F32) + total[c]).astype(BF)
            out_copy(v).start()
            o_ref[pl.ds(mine, ROWS), cols] = ow[v, z_hi]

        @pl.when(o == 1)
        def _():
            for h in (0, 1):
                rows = slice(h * ROWS, (h + 1) * ROWS)
                o_ref[rows, cols] = (3.4445 * x_ref[rows, cols].astype(F32) + total[h]).astype(BF)

    for c in started:
        c.wait_send()

    @pl.when(o == 0)
    def _():
        for v in range(PIECES):
            out_copy(v).wait()


def body(iterate):
    stack = pltpu.VMEM((PIECES, N, ROWS, 2 * PART), BF)
    gram = pltpu.VMEM((N, ROWS, N * ROWS), BF)
    chunks = lambda n: pltpu.VMEM((PIECES, n, ROWS, 2 * PART), BF)
    blocks = lambda n: pltpu.VMEM((PIECES, n, 2, ROWS, PART), BF)
    dma = lambda n: pltpu.SemaphoreType.DMA((2, n))
    return pl.pallas_call(
        kernel,
        out_shape=jax.ShapeDtypeStruct(iterate.shape, BF),
        in_specs=[pl.BlockSpec(memory_space=pl.ANY)],
        out_specs=pl.BlockSpec(memory_space=pltpu.VMEM),
        scratch_shapes=[
            pltpu.VMEM(iterate.shape, BF), pltpu.SemaphoreType.DMA(()),
            pltpu.VMEM((2, 2, N, ROWS, COLS), BF),
            pltpu.VMEM((2, HALF * ROWS, N * ROWS), F32),
            gram, pltpu.VMEM((2, NX - 1, ROWS, N * ROWS), BF), gram,
            pltpu.VMEM((N * ROWS, N * ROWS), BF),
            stack,
            chunks(2), pltpu.VMEM((PIECES, 2, ROWS // 2, 2 * PART), BF), chunks(4), chunks(2),
            stack, pltpu.VMEM((PIECES, ROWS, 2 * PART), F32),
            blocks(N), blocks(2), pltpu.VMEM((PIECES, 2, ROWS, PART), BF), blocks(4), blocks(2),
            pltpu.VMEM((PIECES, 2, ROWS, PART), BF),
            dma(1), dma(16), dma(16), dma(6), dma(6), dma(8 * PIECES), dma(8 * PIECES), dma(8 * PIECES), dma(PIECES),
        ],
        compiler_params=pltpu.CompilerParams(
            collective_id=0, has_side_effects=True, vmem_limit_bytes=40 * 1024 * 1024),
    )(iterate)


def solution(mesh):
    return jax.shard_map(
        body, mesh=mesh,
        in_specs=(P(("layer", "panel"), "col"),),
        out_specs=P(("layer", "panel"), "col"),
        check_vma=False,
    )
```

```python
import jax
import jax.numpy as jnp
from jax import lax
from jax.experimental import pallas as pl
from jax.experimental.pallas import tpu as pltpu
from jax.sharding import PartitionSpec as P

NX, N, NLO = 4, 8, 4
HALF = N // 2
ROWS, COLS = 64, 512
PIECES = 4
PART = COLS // PIECES
ORDER = ((4, 3, 5, 1), (7, 2, 6, 0))
SLOT = {d: k * 4 + i for k in (0, 1) for i, d in enumerate(ORDER[k])}
MESH = pl.DeviceIdType.MESH
BF, F32 = jnp.bfloat16, jnp.float32


def kernel(x_hbm, o_ref, x_ref, x_sem, ab, acc, gp, gr, g, gt, fp, fb, fh, fd, fs, f, first, sp, sb, sh, sd, ss, ow,
           ex_sem, a_sem, b_sem, gr_sem, g_sem, fr_sem, f_sem, sr_sem, out_sem):
    panel, col, layer = lax.axis_index("panel"), lax.axis_index("col"), lax.axis_index("layer")
    y, z_lo = panel // NLO, panel % NLO
    z_hi, x = col // NX, col % NX
    z = z_hi * NLO + z_lo
    o = 1 - layer

    def device(x, y, z):
        return (y * NLO + z % NLO, (z // NLO) * NX + x, layer)

    def place(zz):
        return (zz % NLO) * 2 + zz // NLO

    def ring_y(d):
        return device(x, (y + d + N) % N, z)

    def ring_z(d):
        return device(x, y, (z + d + N) % N)

    def ring1(d):
        return device(x, (y + o * d + N) % N, (z + (1 - o) * d + N) % N)

    def ring2(d):
        return device(x, (y + (1 - o) * d + N) % N, (z + o * d + N) % N)

    def place1(d):
        return (1 - o) * place((z + d + N) % N) + o * ((y + d + N) % N)

    def pos2(d):
        return ((1 - o) * y + o * z + d + N) % N

    def peer_x(d):
        return device((x + d) % NX, y, z)

    partner = device(x, y, (z + HALF) % N)

    barrier = pltpu.get_barrier_semaphore()
    greeted = [device(x, y, (z + HALF) % N)] + [ring(d) for d in (2, -2, 1, -1) for ring in (ring_z, ring_y)]
    greeted += [peer_x(d) for d in (2, 1, 3)]
    for peer in greeted:
        pl.semaphore_signal(barrier, inc=1, device_id=peer, device_id_type=MESH)
    load = pltpu.make_async_copy(x_hbm, x_ref, x_sem)
    load.start()
    pl.semaphore_wait(barrier, len(greeted))
    load.wait()

    def remote(src, dst, send_sem, recv_sem, to):
        return pltpu.make_async_remote_copy(
            src_ref=src, dst_ref=dst, send_sem=send_sem, recv_sem=recv_sem, device_id=to, device_id_type=MESH)

    started = []

    def send(src, dst, send_sem, recv_sem, to):
        copy = remote(src, dst, send_sem, recv_sem, to)
        copy.start()
        started.append(copy)
        return copy

    def gather(slot, ring, sems, base, far):
        def one(code, src, dst, d):
            return send(src, dst, sems.at[0, base + code], sems.at[1, base + code], ring(d))

        second = [one(0, slot(0, 0), slot(0, 2), 2), one(1, slot(0, 0), slot(0, -2), -2)]
        last = [one(2, slot(0, 0), slot(0, 1), 1), one(3, slot(0, 0), slot(0, -1), -1)]
        yield
        for way, sign in ((0, 1), (1, -1)):
            second[way].wait_recv()
            at = -2 * sign
            src, dst = far(way, slot(at, 0)), far(way, slot(at, 2 * sign))
            if src is not None:
                last.append(one(4 + way, src, dst, 2 * sign))
            last.append(one(6 + way, slot(at, 0), slot(at, sign), sign))
        yield
        for copy in last:
            copy.wait_recv()
        yield

    def scatter(parts, index, halves, relay, relay_half, direct, sums, ring, sems, base):
        def one(code, src, dst, d):
            return send(src, dst, sems.at[0, base + code], sems.at[1, base + code], ring(d))

        met, last = [], []
        for way, sign in ((0, -1), (1, 1)):
            met.append([one(way, parts.at[index(4 * sign)].at[halves[way]], relay_half.at[way], 2 * sign)])
        for way, sign in ((0, -1), (1, 1)):
            met[way].append(one(2 + way, parts.at[index(3 * sign)], relay.at[way], sign))
        for way, sign in ((1, 1), (0, -1)):
            last.append(one(4 + way, parts.at[index(sign)], direct.at[way], sign))
            yield
        for way, sign in ((0, -1), (1, 1)):
            for copy in met[way]:
                copy.wait_recv()
            sums[way] = (parts[index(2 * sign)].astype(F32) + relay[way].astype(F32)).astype(BF)
            half = halves[way]
            sums.at[way].at[half][...] = (parts.at[index(2 * sign)].at[half][...].astype(F32) + relay.at[way].at[half][...].astype(F32)
                                + relay_half[way].astype(F32)).astype(BF)
            last.append(one(6 + way, sums.at[way], direct.at[2 + way], 2 * sign))
        yield
        total = parts[index(0)].astype(F32)
        for i, copy in zip((1, 0, 2, 3), last):
            copy.wait_recv()
            total += direct[i].astype(F32)
        yield total

    mine = pl.multiple_of(z_hi * ROWS, ROWS)
    other = pl.multiple_of((1 - z_hi) * ROWS, ROWS)

    exchange = send(x_ref.at[pl.ds(other, ROWS), :], ab.at[1 - o, z_hi, y], ex_sem.at[0, 0], ex_sem.at[1, 0], partner)

    def slot_a(u):
        def slot(d, _):
            zz = (z + d + N) % N
            return ab.at[o, zz // NLO, (zz % NLO) * 2 + u]
        return slot

    def slot_b(c):
        return lambda d, _: ab.at[1 - o, c, (y + d + N) % N]

    row_halves = (pl.ds(0, ROWS // 2), pl.ds(ROWS // 2, ROWS // 2))

    def both(way, ref):
        return ref.at[row_halves[way]]

    c_late = 1 - z_hi
    a0 = gather(slot_a(0), ring_z, a_sem, 0, lambda way, ref: None)
    a1 = gather(slot_a(1), ring_z, a_sem, 8, lambda way, ref: None)
    b0 = gather(slot_b(z_hi), ring_y, b_sem, 0, both)
    b1 = gather(slot_b(c_late), ring_y, b_sem, 8, both)
    ab[1 - o, z_hi, y] = x_ref[pl.ds(mine, ROWS), :]
    next(b0)
    for u in (0, 1):
        ab[o, z_hi, z_lo * 2 + u] = x_ref[u * ROWS:(u + 1) * ROWS, :]
    next(a0)
    next(a1)
    next(b0)
    exchange.wait_recv()
    next(b1)
    next(a0)
    next(a1)
    far = []
    for way, sign in ((0, 1), (1, -1)):
        zz, unseen = (z - 2 * sign + N) % N, 1 - (z + 2 * sign + N) % N // NLO
        part = both(way, ab.at[o, zz // NLO, (zz % NLO) * 2 + unseen])
        far.append(send(part, part, a_sem.at[0, 4 + way], a_sem.at[1, 4 + way], ring_z(2 * sign)))
    ab[o, c_late, z_lo * 2 + z_hi] = ab[1 - o, c_late, y]
    next(b1)
    next(b0)
    next(a0)
    next(a1)
    for copy in far:
        copy.wait_recv()

    def nt(a, b):
        return lax.dot_general(a, b, (((1,), (1,)), ((), ())), preferred_element_type=F32)

    rows_all, rows_half = N * ROWS, HALF * ROWS
    def left(k, c):
        return jnp.concatenate([ab[0, c, place1(d)] for d in ORDER[k]], axis=0)

    for k in (0, 1):
        acc[k] = nt(left(k, z_hi), ab[1, z_hi].reshape(rows_all, COLS))
    next(b1)

    gr_copies = []
    for k in (0, 1):
        block = acc[k] + nt(left(k, c_late), ab[1, c_late].reshape(rows_all, COLS))
        gp[k * HALF:(k + 1) * HALF] = block.astype(BF).reshape(HALF, ROWS, rows_all)
        gr_copies.append([
            send(gp.at[k * HALF + (x + d) % NX], gr.at[k, d - 1], gr_sem.at[0, k * 3 + d - 1],
                 gr_sem.at[1, k * 3 + d - 1], peer_x(d)) for d in (2, 1, 3)])
    g_copies = []
    for k in (0, 1):
        mine_g = k * HALF + x
        for c in gr_copies[k]:
            c.wait_recv()
        total = gp[mine_g].astype(F32)
        for d in range(NX - 1):
            total += gr[k, d].astype(F32)
        g[mine_g] = (total * (1.0 / 4096)).astype(BF)
        g_copies.append([
            send(g.at[mine_g], g.at[mine_g], g_sem.at[0, k * 3 + d - 1], g_sem.at[1, k * 3 + d - 1], peer_x(d))
            for d in (2, 1, 3)])

    firsts = [scatter(fp.at[v], lambda d: SLOT[d % N], row_halves, fb.at[v], fh.at[v], fd.at[v], fs.at[v], ring1, fr_sem, v * 8)
              for v in range(PIECES)]

    def part_of_first(k, v):
        rows = g[k * HALF:(k + 1) * HALF].reshape(rows_half, rows_all)
        for c in (0, 1):
            right = ab[1, c, :, :, v * PART:(v + 1) * PART].reshape(rows_all, PART)
            fp[v, k * HALF:(k + 1) * HALF, :, c * PART:(c + 1) * PART] = jnp.dot(
                rows, right, preferred_element_type=F32).astype(BF).reshape(HALF, ROWS, PART)

    for k in (0, 1):
        for c in g_copies[k]:
            c.wait_recv()
        for v in range(PIECES):
            part_of_first(k, v)
            next(firsts[v])
            if k == 1:
                next(firsts[v])


    gathers = []
    for v in range(PIECES):
        first[v] = next(firsts[v])
        f[v, SLOT[0]] = first[v].astype(BF)
        gathers.append(gather(lambda d, to, v=v: f.at[v, SLOT[(d - to) % N]], ring1, f_sem, v * 8, both))
        next(gathers[v])
    gt[...] = g[...].reshape(rows_all, rows_all).T
    for v in range(PIECES):
        next(gathers[v])


    seconds = [scatter(sp.at[v], pos2, (0, 1), sb.at[v], sh.at[v], sd.at[v], ss.at[v], ring2, sr_sem, v * 8)
               for v in range(PIECES)]
    for v in range(PIECES):
        next(gathers[v])
        second = 2.0315 * jnp.dot(gt[...], f[v].reshape(rows_all, 2 * PART), preferred_element_type=F32)

        @pl.when(o == 0)
        def _():
            for t in range(N):
                for c in (0, 1):
                    part = second[t * ROWS:(t + 1) * ROWS, c * PART:(c + 1) * PART]
                    sp[v, t, c] = part.astype(BF)
            for c in (0, 1):
                sp[v, y, c] = (sp[v, y, c].astype(F32) - 4.775 * first[v, :, c * PART:(c + 1) * PART]).astype(BF)

        @pl.when(o == 1)
        def _():
            for t in range(N):
                for h in (0, 1):
                    at = ((t % NLO) * 2 + h) * ROWS
                    c = t // NLO
                    sp[v, t, h] = second[at:at + ROWS, c * PART:(c + 1) * PART].astype(BF)
            for c in (0, 1):
                at = c * NLO + z_lo
                sp[v, at, z_hi] = (
                    sp[v, at, z_hi].astype(F32) - 4.775 * first[v, :, c * PART:(c + 1) * PART]).astype(BF)

        next(seconds[v])
        next(seconds[v])
    for v in range(PIECES):
        next(seconds[v])

    for c in started[:-2 * PIECES]:
        c.wait_send()
    del started[:-2 * PIECES]

    def out_copy(v):
        return remote(ow.at[v, 1 - z_hi], o_ref.at[pl.ds(mine, ROWS), v * PART:(v + 1) * PART],
                      out_sem.at[0, v], out_sem.at[1, v], partner)

    for v in range(PIECES):
        total = next(seconds[v])
        cols = slice(v * PART, (v + 1) * PART)

        @pl.when(o == 0)
        def _():
            for c in (0, 1):
                ow[v, c] = (3.4445 * ab[1, c, y, :, cols].astype(F32) + total[c]).astype(BF)
            out_copy(v).start()
            o_ref[pl.ds(mine, ROWS), cols] = ow[v, z_hi]

        @pl.when(o == 1)
        def _():
            for h in (0, 1):
                rows = slice(h * ROWS, (h + 1) * ROWS)
                o_ref[rows, cols] = (3.4445 * x_ref[rows, cols].astype(F32) + total[h]).astype(BF)

    for c in started:
        c.wait_send()

    @pl.when(o == 0)
    def _():
        for v in range(PIECES):
            out_copy(v).wait()


def body(iterate):
    stack = pltpu.VMEM((PIECES, N, ROWS, 2 * PART), BF)
    gram = pltpu.VMEM((N, ROWS, N * ROWS), BF)
    chunks = lambda n: pltpu.VMEM((PIECES, n, ROWS, 2 * PART), BF)
    blocks = lambda n: pltpu.VMEM((PIECES, n, 2, ROWS, PART), BF)
    dma = lambda n: pltpu.SemaphoreType.DMA((2, n))
    return pl.pallas_call(
        kernel,
        out_shape=jax.ShapeDtypeStruct(iterate.shape, BF),
        in_specs=[pl.BlockSpec(memory_space=pl.ANY)],
        out_specs=pl.BlockSpec(memory_space=pltpu.VMEM),
        scratch_shapes=[
            pltpu.VMEM(iterate.shape, BF), pltpu.SemaphoreType.DMA(()),
            pltpu.VMEM((2, 2, N, ROWS, COLS), BF),
            pltpu.VMEM((2, HALF * ROWS, N * ROWS), F32),
            gram, pltpu.VMEM((2, NX - 1, ROWS, N * ROWS), BF), gram,
            pltpu.VMEM((N * ROWS, N * ROWS), BF),
            stack,
            chunks(2), pltpu.VMEM((PIECES, 2, ROWS // 2, 2 * PART), BF), chunks(4), chunks(2),
            stack, pltpu.VMEM((PIECES, ROWS, 2 * PART), F32),
            blocks(N), blocks(2), pltpu.VMEM((PIECES, 2, ROWS, PART), BF), blocks(4), blocks(2),
            pltpu.VMEM((PIECES, 2, ROWS, PART), BF),
            dma(1), dma(16), dma(16), dma(6), dma(6), dma(8 * PIECES), dma(8 * PIECES), dma(8 * PIECES), dma(PIECES),
        ],
        compiler_params=pltpu.CompilerParams(
            collective_id=0, has_side_effects=True, vmem_limit_bytes=40 * 1024 * 1024),
    )(iterate)


def solution(mesh):
    return jax.shard_map(
        body, mesh=mesh,
        in_specs=(P(("layer", "panel"), "col"),),
        out_specs=P(("layer", "panel"), "col"),
        check_vma=False,
    )
```
